32 devices in a mesh: grp: 2 (over x), res: 16 (over z, y, core).
Axes of the slice: x: 2, y: 2, z: 4, core: 2. Of those that a mesh axis runs over, the one named last changes fastest.
Arguments:
- queries: bfloat16 [8192, 512], P(('grp', 'res')), parts along dimension 0, may hold values from -6 to 6
- query_points: bfloat16 [8192, 384], P(('grp', 'res')), parts along dimension 0, may hold values from -5 to 8
- keys: bfloat16 [8192, 512], P(('grp', 'res')), parts along dimension 0, may hold values from -6 to 6
- key_points: bfloat16 [8192, 384], P(('grp', 'res')), parts along dimension 0, may hold values from -6 to 6
- values: bfloat16 [8192, 512], P(('grp', 'res')), parts along dimension 0, may hold values from -6 to 6
- point_weights: float32 [16], replicated, may hold values from 0.3 to 3
- out_grad: bfloat16 [8192, 512], P(('grp', 'res')), parts along dimension 0, may hold values from -6 to 6
- fetch_block: int32 [32, 16], P(('grp', 'res')), parts along dimension 0, may hold values from 0 to 1
- key_owner: int32 [64, 16], P(('grp', 'res')), parts along dimension 0, may hold values from 0 to 15, as said below
- key_live: int32 [64, 16], P(('grp', 'res')), parts along dimension 0, may hold values from 0 to 1, as said below
Outputs:
- query_grad: float32 [8192, 512], P(('grp', 'res')), parts along dimension 0
- query_point_grad: float32 [8192, 384], P(('grp', 'res')), parts along dimension 0
- key_grad: float32 [8192, 512], P(('grp', 'res')), parts along dimension 0
- key_point_grad: float32 [8192, 384], P(('grp', 'res')), parts along dimension 0
- value_grad: float32 [8192, 512], P(('grp', 'res')), parts along dimension 0
The draws below stay inside these ranges and needn't reach their ends.
There are 2 independent parts, one for each index of `grp`. The reference program is written for one: setup_inputs(seed, part) draws one part's arguments, and reference() takes and returns one part's arrays. A program takes and returns all parts, laid end to end along the dimension named above; an argument that names none is the same for every part. Nothing has to cross between parts.
Inputs may be any that keep to these rules, and one draw needn't show every extreme that they name: `key_owner`: the 16 entries of one query block name distinct devices. `key_live`: in each row the live slots come first; a row has 4 to 16 of them, and row 0 has all.
All inputs are finite; a program needn't handle non-finite values.
Results may differ from the reference program's by a relative error of at most 0.012.
The reference program's roundings to bfloat16 on the way (of `probs_low` and `score_low`) count: a program that leaves them out, or rounds other values in their place, can miss the bound.
Values may be sent and summed in bfloat16 or wider, within the bound.
A program may use at most 192 MiB of HBM per device.

```python
import math
import jax
import jax.numpy as jnp
from jax import lax

HEADS = 16
BLOCK = 128
NEIGHBOURS = 16
QBLOCKS = 2
RESIDUES = 4096
NBLOCKS = 32
WIDTH = 512
PWIDTH = 384
FEAT = 1408
N_RES = 16


def draw_query_points(random_key, part_index):
    random_key = jax.random.fold_in(random_key, 11)
    shape = (RESIDUES, PWIDTH)
    return jnp.clip(jax.random.normal(random_key, shape, jnp.float32), -5.0, 5.0).astype(jnp.bfloat16)


def pick_owners(row_key):
    return jax.random.permutation(row_key, N_RES)[:NEIGHBOURS]


def draw_key_owner(random_key, part_index):
    random_key = jax.random.fold_in(random_key, 23)
    row_keys = jax.random.split(random_key, NBLOCKS)
    return jax.vmap(pick_owners)(row_keys).astype(jnp.int32)


def draw_key_live(random_key, part_index):
    random_key = jax.random.fold_in(random_key, 37)
    counts = jax.random.randint(random_key, (NBLOCKS,), NEIGHBOURS // 4, NEIGHBOURS + 1)
    counts = counts.at[0].set(NEIGHBOURS)
    slot_index = jnp.arange(NEIGHBOURS, dtype=jnp.int32)
    return (slot_index[None, :] < counts[:, None]).astype(jnp.int32)


def with_ends(entries, key, low, top_value):
    longest = entries.shape.index(max(entries.shape))
    spots = []
    for shift in (0, 1):
        where = [jax.random.randint(jax.random.fold_in(key, axis), (), 0, length) for axis, length in enumerate(entries.shape)]
        where[longest] = (where[longest] + shift) % entries.shape[longest]
        spots.append(tuple(where))
    return entries.at[spots[0]].set(low).at[spots[1]].set(top_value)


def block_levels(key, dims, pieces, low, high):
    gain, own = 1.0, jax.random.fold_in(key, 6)
    for axis_at, blocks in pieces:
        steps = jnp.exp(jax.random.uniform(jax.random.fold_in(own, axis_at), (blocks,), jnp.float32, low / len(pieces), high / len(pieces)))
        gain = gain * jnp.repeat(steps, dims[axis_at] // blocks).reshape([-1 if axis == axis_at else 1 for axis in range(len(dims))])
    return gain


def gaussian(own_key, dims, scale, bound, shards=(), kind=jnp.bfloat16):
    values = scale * jax.random.normal(own_key, dims, jnp.float32)
    if shards:
        values = values * block_levels(own_key, dims, shards, -0.22, 0.18)
    return jnp.clip(values, -bound, bound).astype(kind)


def setup_inputs(seed: int = 0, part: int = 0) -> dict:
    key_of = jax.random.split(jax.random.key(seed), 11)
    own_keys = jax.random.split(jax.random.fold_in(key_of[10], part), 11)
    return {
        "queries": gaussian(own_keys[0], (RESIDUES, WIDTH), 1.0, 6.0, ((0, 16),)),
        "query_points": draw_query_points(jax.random.fold_in(jax.random.fold_in(key_of[10], part), 71), part),
        "keys": gaussian(own_keys[2], (RESIDUES, WIDTH), 1.0, 6.0, ((0, 16),)),
        "key_points": gaussian(own_keys[3], (RESIDUES, PWIDTH), 1.0, 6.0, ((0, 16),)),
        "values": gaussian(own_keys[4], (RESIDUES, WIDTH), 1.0, 6.0, ((0, 16),)),
        "point_weights": jnp.clip(jnp.exp(jax.random.uniform(key_of[5], (HEADS,), jnp.float32, math.log(0.3), math.log(3.0))), 0.3, 3.0),
        "out_grad": gaussian(own_keys[6], (RESIDUES, WIDTH), 1.0, 6.0, ((0, 16),)),
        "fetch_block": with_ends(jax.random.randint(own_keys[7], (N_RES, N_RES), 0, QBLOCKS), jax.random.fold_in(own_keys[7], 1), 0, QBLOCKS - 1).astype(jnp.int32),
        "key_owner": draw_key_owner(jax.random.fold_in(jax.random.fold_in(key_of[10], part), 71), part),
        "key_live": draw_key_live(jax.random.fold_in(jax.random.fold_in(key_of[10], part), 71), part),
    }


LOGIT_WEIGHT = math.sqrt(1.0 / 3.0)

def round_low(values_in):
    narrowed = values_in.astype(jnp.bfloat16)
    narrowed = lax.optimization_barrier(narrowed)
    return narrowed.astype(jnp.float32)

def block_grads(query_block, query_pts, cot_block, gathered, live_cols, weights):
    row_count = query_block.shape[0]
    model_width = query_block.shape[1]
    head_count = weights.shape[0]
    head_dim = model_width // head_count
    points = query_pts.shape[1] // (3 * head_count)
    key_count = gathered.shape[0]
    wide = gathered.astype(jnp.float32)
    key_part = wide[:, :model_width].reshape(key_count, head_count, head_dim)
    value_part = wide[:, model_width:2 * model_width].reshape(key_count, head_count, head_dim)
    key_grid = wide[:, 2 * model_width:].reshape(key_count, 3, head_count, points)
    query_heads = query_block.astype(jnp.float32).reshape(row_count, head_count, head_dim)
    cot_heads = cot_block.astype(jnp.float32).reshape(row_count, head_count, head_dim)
    query_grid = query_pts.astype(jnp.float32).reshape(row_count, 3, head_count, points)
    scalar_scale = LOGIT_WEIGHT / math.sqrt(head_dim)
    point_scale = LOGIT_WEIGHT * math.sqrt(2.0 / (9.0 * points)) * weights
    scores = jnp.einsum('bhc,mhc->hbm', query_heads, key_part)
    crossed = jnp.einsum('bxhp,mxhp->hbm', query_grid, key_grid)
    query_sq = lax.optimization_barrier(jnp.sum(query_grid * query_grid, axis=(1, 3))).T
    key_sq = lax.optimization_barrier(jnp.sum(key_grid * key_grid, axis=(1, 3))).T
    distance = query_sq[:, :, None] + key_sq[:, None, :] - 2.0 * crossed
    logits = scalar_scale * scores - 0.5 * point_scale[:, None, None] * distance
    logits = jnp.where(live_cols[None, None, :], logits, -jnp.inf)
    highest = lax.optimization_barrier(jnp.max(logits, axis=2, keepdims=True))
    exponent = jnp.exp(logits - highest)
    softmax_weights = exponent / lax.optimization_barrier(jnp.sum(exponent, axis=2, keepdims=True))
    probs_low = round_low(softmax_weights)
    attended = jnp.einsum('hbm,mhc->bhc', probs_low, value_part)
    delta_term = lax.optimization_barrier(jnp.sum(cot_heads * attended, axis=2)).T
    prob_grad = jnp.einsum('bhc,mhc->hbm', cot_heads, value_part)
    score_grad = softmax_weights * (prob_grad - delta_term[:, :, None])
    score_low = round_low(score_grad)
    query_grad = scalar_scale * jnp.einsum('hbm,mhc->bhc', score_low, key_part)
    row_total = lax.optimization_barrier(jnp.sum(score_grad, axis=2)).T
    point_pull = jnp.einsum('hbm,mxhp->bxhp', score_low, key_grid)
    query_point_grad = -point_scale[None, None, :, None] * (row_total[:, None, :, None] * query_grid - point_pull)
    key_grad = scalar_scale * jnp.einsum('hbm,bhc->mhc', score_low, query_heads)
    col_total = lax.optimization_barrier(jnp.sum(score_grad, axis=1)).T
    key_pull = jnp.einsum('hbm,bxhp->mxhp', score_low, query_grid)
    key_point_grad = point_scale[None, None, :, None] * (key_pull - col_total[:, None, :, None] * key_grid)
    value_grad = jnp.einsum('hbm,bhc->mhc', probs_low, cot_heads)
    slot_terms = jnp.concatenate([key_grad.reshape(key_count, model_width), value_grad.reshape(key_count, model_width), key_point_grad.reshape(key_count, -1)], axis=1)
    return (query_grad.reshape(row_count, model_width), query_point_grad.reshape(row_count, -1), slot_terms)

def reference(queries, query_points, keys, key_points, values, point_weights, out_grad, fetch_block, key_owner, key_live):
    packed = jnp.concatenate([keys, values, key_points], axis=1).reshape(NBLOCKS, BLOCK, FEAT)
    owner_ids = jnp.arange(N_RES, dtype=jnp.int32)

    def per_device(running, inputs):
        query_dev, point_dev, cot_dev, fetch_row, owner_dev, live_dev = inputs
        targets = (owner_ids * QBLOCKS + fetch_row).astype(jnp.int32)
        slot_blocks = packed[targets]

        def per_block(slot_sums, block_inputs):
            query_block, query_pts, cot_block, owner_row, live_row = block_inputs
            gathered = slot_blocks[owner_row].reshape(NEIGHBOURS * BLOCK, FEAT)
            live_cols = jnp.repeat(live_row > 0, BLOCK)
            query_grad, point_grad, slot_terms = block_grads(query_block, query_pts, cot_block, gathered, live_cols, point_weights)
            slot_sums = slot_sums.at[owner_row].add(slot_terms.reshape(NEIGHBOURS, BLOCK, FEAT))
            return (slot_sums, (query_grad, point_grad))
        slot_sums, block_outs = lax.scan(per_block, jnp.zeros((N_RES, BLOCK, FEAT), jnp.float32), (query_dev, point_dev, cot_dev, owner_dev, live_dev))
        running = running.at[targets].add(round_low(slot_sums))
        return (running, block_outs)
    inputs = (queries.reshape(N_RES, QBLOCKS, BLOCK, WIDTH), query_points.reshape(N_RES, QBLOCKS, BLOCK, PWIDTH), out_grad.reshape(N_RES, QBLOCKS, BLOCK, WIDTH), fetch_block, key_owner.reshape(N_RES, QBLOCKS, NEIGHBOURS), key_live.reshape(N_RES, QBLOCKS, NEIGHBOURS))
    totals, (query_grads, point_grads) = lax.scan(per_device, jnp.zeros((NBLOCKS, BLOCK, FEAT), jnp.float32), inputs)
    totals = totals.reshape(RESIDUES, FEAT)
    return (query_grads.reshape(RESIDUES, WIDTH), point_grads.reshape(RESIDUES, PWIDTH), totals[:, :WIDTH], totals[:, 2 * WIDTH:], totals[:, WIDTH:2 * WIDTH])
```

```python
import functools
import math

import jax
import jax.numpy as jnp
from jax import lax
from jax.experimental import pallas as pl
from jax.experimental.pallas import tpu as pltpu
from jax.sharding import PartitionSpec as P

BLOCK = 128
LOGIT_WEIGHT = math.sqrt(1.0 / 3.0)
HEAD_COLS = 64
QUAD = 4
CHUNK = 2 * BLOCK
F32 = jnp.float32
BF16 = jnp.bfloat16


def dot(a, b):
    return jnp.dot(a, b, preferred_element_type=F32)


def fold(x, op):
    return op(x.reshape(x.shape[0] // 8, 8, x.shape[1]), axis=0)


def attention_kernel(
    head_dim, point_cols, kx_ref, v_ref, qhi_ref, qlo_ref, qraw_ref, cot_ref, cott_ref, qt_ref,
    bias_ref, colscale_ref, colpoint_ref, rowscale_ref, rowpoint_ref,
    kterm_ref, vterm_ref, qgrad_ref, s_ref, d_ref,
):
    keys = kx_ref.shape[0]
    cols = qhi_ref.shape[1]
    chunks = keys // CHUNK
    zeros = jnp.zeros((HEAD_COLS, cols), BF16)

    def score_weights(h):
        rows = slice(h * HEAD_COLS, (h + 1) * HEAD_COLS)
        hi, lo = qhi_ref[rows, :], qlo_ref[rows, :]
        parts = [hi, zeros, lo, zeros] if h % 2 == 0 else [zeros, hi, zeros, lo]
        return jnp.concatenate(parts, axis=0)

    def cot_weights(h):
        row = lax.broadcasted_iota(jnp.int32, (QUAD * head_dim, cols), 0)
        keep = (row >= h * head_dim) & (row < (h + 1) * head_dim)
        return jnp.where(keep, cott_ref[...], jnp.zeros((), BF16))

    qw = [score_weights(h) for h in range(QUAD)]
    ow = [cot_weights(h) for h in range(QUAD)]

    def scores(i, highest):
        rows = pl.ds(pl.multiple_of(i * CHUNK, CHUNK), CHUNK)
        low = bias_ref[pl.ds(i * 2, 1), :]
        high = bias_ref[pl.ds(i * 2 + 1, 1), :]
        vals = v_ref[rows, :]
        out = []
        for h in range(QUAD):
            pair = kx_ref[rows, (h // 2) * 128 : (h // 2 + 1) * 128]
            s = dot(jnp.concatenate([pair, pair], axis=1), qw[h])
            s = jnp.concatenate([s[:BLOCK] + low, s[BLOCK:] + high], axis=0)
            s_ref[h, rows, :] = s
            out.append(jnp.maximum(highest[h], fold(s, jnp.max)))
            d_ref[h, rows, :] = dot(vals, ow[h])
        return tuple(out)

    highest = lax.fori_loop(
        0, chunks, scores, tuple(jnp.full((8, cols), -jnp.inf, F32) for _ in range(QUAD))
    )
    highest = [jnp.max(x, axis=0, keepdims=True) for x in highest]

    def exps(i, total):
        rows = pl.ds(pl.multiple_of(i * CHUNK, CHUNK), CHUNK)
        out = []
        for h in range(QUAD):
            e = jnp.exp(s_ref[h, rows, :] - highest[h])
            s_ref[h, rows, :] = e
            out.append(total[h] + fold(e, jnp.sum))
        return tuple(out)

    zero8 = tuple(jnp.zeros((8, cols), F32) for _ in range(QUAD))
    total = lax.fori_loop(0, chunks, exps, zero8)
    inverse = [1.0 / jnp.sum(x, axis=0, keepdims=True) for x in total]

    def deltas(i, delta):
        rows = pl.ds(pl.multiple_of(i * CHUNK, CHUNK), CHUNK)
        out = []
        for h in range(QUAD):
            p = s_ref[h, rows, :] * inverse[h]
            low = p.astype(BF16).astype(F32)
            out.append(delta[h] + fold(low * d_ref[h, rows, :], jnp.sum))
        return tuple(out)

    delta = lax.fori_loop(0, chunks, deltas, zero8)
    delta = [jnp.sum(x, axis=0, keepdims=True) for x in delta]

    lane = lax.broadcasted_iota(jnp.int32, (cols, 128), 1)
    qk = []
    ok = []
    for h in range(QUAD):
        pair = qraw_ref[:, (h // 2) * 128 : (h // 2 + 1) * 128]
        qk.append(jnp.where(lane // HEAD_COLS == h % 2, pair, jnp.zeros((), BF16)))
        ok.append(jnp.where(lane // head_dim == h, cot_ref[...], jnp.zeros((), BF16)))
    half = lax.broadcasted_iota(jnp.int32, (CHUNK, 128), 1) < HEAD_COLS

    def grads(i, carry):
        row_total, pulls = carry
        rows = pl.ds(pl.multiple_of(i * CHUNK, CHUNK), CHUNK)
        new_total, new_pulls = [], []
        vterm = None
        for g in range(QUAD // 2):
            pair = kx_ref[rows, g * 128 : (g + 1) * 128]
            kterm = None
            col_totals = []
            for h in (2 * g, 2 * g + 1):
                p = s_ref[h, rows, :] * inverse[h]
                p_low = p.astype(BF16)
                ds = p * (d_ref[h, rows, :] - delta[h])
                ds_low = ds.astype(BF16)
                new_total.append(row_total[h] + fold(ds, jnp.sum))
                col_totals.append(jnp.sum(ds, axis=1, keepdims=True))
                kt = dot(ds_low, qk[h])
                kterm = kt if kterm is None else kterm + kt
                vt = dot(p_low, ok[h])
                vterm = vt if vterm is None else vterm + vt
                pull = lax.dot_general(
                    pair, ds_low, (((0,), (0,)), ((), ())), preferred_element_type=F32
                )
                off = (h % 2) * HEAD_COLS
                new_pulls.append(pulls[h] + pull[off : off + HEAD_COLS])
            sums = jnp.where(half, col_totals[0], col_totals[1])
            span = slice(g * 128, (g + 1) * 128)
            kterm = colscale_ref[:, span] * kterm - colpoint_ref[:, span] * sums * pair.astype(F32)
            kterm_ref[rows, span] = kterm.astype(BF16)
        vterm_ref[rows, :] = vterm.astype(BF16)
        return tuple(new_total), tuple(new_pulls)

    pull0 = tuple(jnp.zeros((HEAD_COLS, cols), F32) for _ in range(QUAD))
    row_total, pulls = lax.fori_loop(0, chunks, grads, (zero8, pull0))
    for h in range(QUAD):
        rows = slice(h * HEAD_COLS, (h + 1) * HEAD_COLS)
        total_h = jnp.sum(row_total[h], axis=0, keepdims=True)
        qgrad_ref[rows, :] = (
            rowscale_ref[rows, :] * pulls[h]
            - rowpoint_ref[rows, :] * total_h * qt_ref[rows, :].astype(F32)
        )


def attention(kx, vals, qhi, qlo, qraw, cot, cott, qt, bias, vecs, head_dim, point_cols):
    keys = kx.shape[0]
    heads = kx.shape[1] // HEAD_COLS
    cols = qhi.shape[1]
    kw, vw = QUAD * HEAD_COLS, QUAD * head_dim
    colscale, colpoint = vecs
    by_col = lambda rows, width: pl.BlockSpec((rows, width), lambda i: (0, i))
    by_row = lambda height, width: pl.BlockSpec((height, width), lambda i: (i, 0))
    return pl.pallas_call(
        functools.partial(attention_kernel, head_dim, point_cols),
        grid=(heads // QUAD,),
        in_specs=[
            by_col(keys, kw), by_col(keys, vw), by_row(kw, cols), by_row(kw, cols),
            by_col(cols, kw), by_col(cols, vw), by_row(vw, cols), by_row(kw, cols),
            pl.BlockSpec(bias.shape, lambda i: (0, 0)),
            by_col(1, kw), by_col(1, kw), by_row(kw, 1), by_row(kw, 1),
        ],
        out_specs=[by_col(keys, kw), by_col(keys, vw), by_row(kw, cols)],
        out_shape=[
            jax.ShapeDtypeStruct((keys, heads * HEAD_COLS), BF16),
            jax.ShapeDtypeStruct((keys, heads * head_dim), BF16),
            jax.ShapeDtypeStruct((heads * HEAD_COLS, cols), F32),
        ],
        scratch_shapes=[
            pltpu.VMEM((QUAD, keys, cols), F32),
            pltpu.VMEM((QUAD, keys, cols), F32),
        ],
        compiler_params=pltpu.CompilerParams(vmem_limit_bytes=60 * 1024 * 1024),
        name="attention",
    )(kx, vals, qhi, qlo, qraw, cot, cott, qt, bias, colscale, colpoint,
      colscale.reshape(-1, 1), colpoint.reshape(-1, 1))


def split2(x):
    hi = lax.reduce_precision(x, 8, 7)
    return hi.astype(BF16), (x - hi).astype(BF16)


def head_layout(scalars, points, heads, extra):
    rows = scalars.shape[0]
    head_dim = scalars.shape[1] // heads
    count = points.shape[1] // (3 * heads)
    grid = points.reshape(rows, 3, heads, count).transpose(0, 2, 1, 3).reshape(rows, heads, 3 * count)
    pad = jnp.zeros((rows, heads, HEAD_COLS - head_dim - 3 * count - extra.shape[2]), scalars.dtype)
    parts = [scalars.reshape(rows, heads, head_dim), grid, extra, pad]
    return jnp.concatenate(parts, axis=2).reshape(rows, heads * HEAD_COLS)


def prepare(queries, query_points, keys, key_points, weights, out_grad):
    heads = weights.shape[0]
    rows, width = queries.shape
    head_dim = width // heads
    count = query_points.shape[1] // (3 * heads)
    scalar_scale = LOGIT_WEIGHT / math.sqrt(head_dim)
    point_scale = LOGIT_WEIGHT * math.sqrt(2.0 / (9.0 * count)) * weights
    wide = key_points.astype(F32).reshape(rows, 3, heads, count)
    ksq = jnp.sum(wide * wide, axis=(1, 3))
    k1 = lax.reduce_precision(ksq, 8, 7)
    k2 = lax.reduce_precision(ksq - k1, 8, 7)
    k3 = ksq - k1 - k2
    pieces = jnp.stack([k1, k2, k3], axis=2).astype(BF16)
    kx = head_layout(keys, key_points, heads, pieces)
    qraw = head_layout(queries, query_points, heads, jnp.zeros((rows, heads, 3), BF16))
    qt = qraw.T
    slot = jnp.arange(HEAD_COLS)
    is_scalar = slot < head_dim
    is_point = (slot >= head_dim) & (slot < head_dim + 3 * count)
    is_square = (slot >= head_dim + 3 * count) & (slot < head_dim + 3 * count + 3)
    a = point_scale[:, None]
    colscale = jnp.where(is_scalar, scalar_scale, jnp.where(is_point, a, 0.0)).reshape(1, -1)
    colpoint = jnp.where(is_point, a, 0.0).reshape(1, -1)
    square = jnp.where(is_square, -0.5 * a, 0.0).reshape(-1, 1)
    qhi, qlo = split2(qt.astype(F32) * colscale.reshape(-1, 1) + square)
    return kx, qraw, qt, qhi, qlo, out_grad.T, (colscale, colpoint)


def unlayout(x, heads, head_dim, count):
    rows = x.shape[0]
    x = x.reshape(rows, heads, HEAD_COLS)
    points = x[:, :, head_dim : head_dim + 3 * count].reshape(rows, heads, 3, count)
    return (
        x[:, :, :head_dim].reshape(rows, heads * head_dim),
        points.transpose(0, 2, 1, 3).reshape(rows, 3 * heads * count),
    )


def local(
    queries, query_points, keys, key_points, values, point_weights, out_grad,
    fetch_block, key_owner, key_live,
):
    owners = lax.axis_size("res")
    rows, width = queries.shape
    blocks = rows // BLOCK
    heads = point_weights.shape[0]
    head_dim = width // heads
    count = query_points.shape[1] // (3 * heads)
    kx, qraw, qt, qhi, qlo, cott, vecs = prepare(
        queries, query_points, keys, key_points, point_weights, out_grad
    )
    owner_ids = jnp.arange(owners, dtype=jnp.int32)
    named = (key_owner[:, :, None] == owner_ids) & (key_live > 0)[:, :, None]
    live = jnp.any(named, axis=1)
    bias = jnp.repeat(jnp.where(live, 0.0, -jnp.inf).astype(F32).T, BLOCK, axis=1)

    request_table = lax.all_gather(fetch_block, "res", axis=0, tiled=True)
    wanted = lax.dynamic_slice_in_dim(request_table, lax.axis_index("res"), 1, 1)[:, 0]
    packed = jnp.concatenate([kx, values], axis=1).reshape(blocks, BLOCK, -1)
    features = packed.shape[2]
    outgoing = jnp.take(packed, wanted, axis=0)
    fetched = lax.all_to_all(outgoing, "res", split_axis=0, concat_axis=0, tiled=True)
    fetched = fetched.reshape(owners * BLOCK, features)
    split = heads * HEAD_COLS
    kterm, vterm, qgrad = attention(
        fetched[:, :split], fetched[:, split:], qhi, qlo, qraw, out_grad, cott, qt, bias, vecs,
        head_dim, 3 * count,
    )
    terms = jnp.concatenate([kterm, vterm], axis=1).reshape(owners, 1, BLOCK, features)
    block_ids = jnp.arange(blocks, dtype=jnp.int32)
    chosen = (fetch_block[0][:, None] == block_ids)[:, :, None, None]
    sent = jnp.where(chosen, terms, jnp.zeros((), BF16)).reshape(owners * rows, features)
    summed = lax.psum_scatter(sent, "res", scatter_dimension=0, tiled=True).astype(F32)
    query_grad, query_point_grad = unlayout(qgrad.T, heads, head_dim, count)
    key_grad, key_point_grad = unlayout(summed[:, :split], heads, head_dim, count)
    return query_grad, query_point_grad, key_grad, key_point_grad, summed[:, split:]


def solution(mesh):
    rows = P(("grp", "res"), None)
    return jax.shard_map(
        local,
        mesh=mesh,
        in_specs=(rows,) * 5 + (P(),) + (rows,) * 4,
        out_specs=(rows,) * 5,
        check_vma=False,
    )
```

```python
import functools
import math

import jax
import jax.numpy as jnp
from jax import lax
from jax.experimental import pallas as pl
from jax.experimental.pallas import tpu as pltpu
from jax.sharding import PartitionSpec as P

BLOCK = 128
LOGIT_WEIGHT = math.sqrt(1.0 / 3.0)
HEAD_COLS = 64
QUAD = 4
CHUNK = 2 * BLOCK
F32 = jnp.float32
BF16 = jnp.bfloat16


def dot(a, b):
    return jnp.dot(a, b, preferred_element_type=F32)


def fold(x, op):
    return op(x.reshape(x.shape[0] // 8, 8, x.shape[1]), axis=0)


def attention_kernel(
    head_dim, pick_ref, g_ref, qhi_ref, qlo_ref, qraw_ref, cot_ref, cott_ref, qt_ref,
    bias_ref, colscale_ref, colpoint_ref, rowscale_ref, rowpoint_ref,
    term_ref, qgrad_ref, s_ref, d_ref,
):
    keys = s_ref.shape[1]
    wide = QUAD * HEAD_COLS
    cols = qhi_ref.shape[1]
    chunks = keys // CHUNK
    zeros = jnp.zeros((HEAD_COLS, cols), BF16)

    def score_weights(h):
        rows = slice(h * HEAD_COLS, (h + 1) * HEAD_COLS)
        hi, lo = qhi_ref[rows, :], qlo_ref[rows, :]
        parts = [hi, zeros, lo, zeros] if h % 2 == 0 else [zeros, hi, zeros, lo]
        return jnp.concatenate(parts, axis=0)

    def cot_weights(h):
        row = lax.broadcasted_iota(jnp.int32, (QUAD * head_dim, cols), 0)
        keep = (row >= h * head_dim) & (row < (h + 1) * head_dim)
        return jnp.where(keep, cott_ref[...], jnp.zeros((), BF16))

    def load(i, span):
        first = g_ref[0, 2 * i, pick_ref[2 * i], :, span]
        second = g_ref[0, 2 * i + 1, pick_ref[2 * i + 1], :, span]
        return jnp.concatenate([first, second], axis=0)

    def store(i, span, value):
        for j in range(2):
            o = 2 * i + j
            part = value[j * BLOCK : (j + 1) * BLOCK].astype(BF16)
            term_ref[0, o, pick_ref[o], :, span] = part
            term_ref[0, o, 1 - pick_ref[o], :, span] = jnp.zeros_like(part)

    qw = [score_weights(h) for h in range(QUAD)]
    ow = [cot_weights(h) for h in range(QUAD)]

    def scores(i, highest):
        rows = pl.ds(pl.multiple_of(i * CHUNK, CHUNK), CHUNK)
        low = bias_ref[pl.ds(i * 2, 1), :]
        high = bias_ref[pl.ds(i * 2 + 1, 1), :]
        vals = load(i, slice(wide, wide + 128))
        out = []
        for h in range(QUAD):
            pair = load(i, slice((h // 2) * 128, (h // 2 + 1) * 128))
            s = dot(jnp.concatenate([pair, pair], axis=1), qw[h])
            s = jnp.concatenate([s[:BLOCK] + low, s[BLOCK:] + high], axis=0)
            s_ref[h, rows, :] = s
            out.append(jnp.maximum(highest[h], fold(s, jnp.max)))
            d_ref[h, rows, :] = dot(vals, ow[h])
        return tuple(out)

    highest = lax.fori_loop(
        0, chunks, scores, tuple(jnp.full((8, cols), -jnp.inf, F32) for _ in range(QUAD))
    )
    highest = [jnp.max(x, axis=0, keepdims=True) for x in highest]

    def exps(i, total):
        rows = pl.ds(pl.multiple_of(i * CHUNK, CHUNK), CHUNK)
        out = []
        for h in range(QUAD):
            e = jnp.exp(s_ref[h, rows, :] - highest[h])
            s_ref[h, rows, :] = e
            out.append(total[h] + fold(e, jnp.sum))
        return tuple(out)

    zero8 = tuple(jnp.zeros((8, cols), F32) for _ in range(QUAD))
    total = lax.fori_loop(0, chunks, exps, zero8)
    inverse = [1.0 / jnp.sum(x, axis=0, keepdims=True) for x in total]

    def deltas(i, delta):
        rows = pl.ds(pl.multiple_of(i * CHUNK, CHUNK), CHUNK)
        out = []
        for h in range(QUAD):
            p = s_ref[h, rows, :] * inverse[h]
            low = p.astype(BF16).astype(F32)
            out.append(delta[h] + fold(low * d_ref[h, rows, :], jnp.sum))
        return tuple(out)

    delta = lax.fori_loop(0, chunks, deltas, zero8)
    delta = [jnp.sum(x, axis=0, keepdims=True) for x in delta]

    lane = lax.broadcasted_iota(jnp.int32, (cols, 128), 1)
    qk = []
    ok = []
    for h in range(QUAD):
        pair = qraw_ref[:, (h // 2) * 128 : (h // 2 + 1) * 128]
        qk.append(jnp.where(lane // HEAD_COLS == h % 2, pair, jnp.zeros((), BF16)))
        ok.append(jnp.where(lane // head_dim == h, cot_ref[...], jnp.zeros((), BF16)))
    half = lax.broadcasted_iota(jnp.int32, (CHUNK, 128), 1) < HEAD_COLS

    def grads(i, carry):
        row_total, pulls = carry
        rows = pl.ds(pl.multiple_of(i * CHUNK, CHUNK), CHUNK)
        new_total, new_pulls = [], []
        vterm = None
        for g in range(QUAD // 2):
            pair = load(i, slice(g * 128, (g + 1) * 128))
            kterm = None
            col_totals = []
            for h in (2 * g, 2 * g + 1):
                p = s_ref[h, rows, :] * inverse[h]
                p_low = p.astype(BF16)
                ds = p * (d_ref[h, rows, :] - delta[h])
                ds_low = ds.astype(BF16)
                new_total.append(row_total[h] + fold(ds, jnp.sum))
                col_totals.append(jnp.sum(ds, axis=1, keepdims=True))
                kt = dot(ds_low, qk[h])
                kterm = kt if kterm is None else kterm + kt
                vt = dot(p_low, ok[h])
                vterm = vt if vterm is None else vterm + vt
                pull = lax.dot_general(
                    pair, ds_low, (((0,), (0,)), ((), ())), preferred_element_type=F32
                )
                off = (h % 2) * HEAD_COLS
                new_pulls.append(pulls[h] + pull[off : off + HEAD_COLS])
            sums = jnp.where(half, col_totals[0], col_totals[1])
            span = slice(g * 128, (g + 1) * 128)
            kterm = colscale_ref[:, span] * kterm - colpoint_ref[:, span] * sums * pair.astype(F32)
            store(i, span, kterm)
        store(i, slice(wide, wide + 128), vterm)
        return tuple(new_total), tuple(new_pulls)

    pull0 = tuple(jnp.zeros((HEAD_COLS, cols), F32) for _ in range(QUAD))
    row_total, pulls = lax.fori_loop(0, chunks, grads, (zero8, pull0))
    for h in range(QUAD):
        rows = slice(h * HEAD_COLS, (h + 1) * HEAD_COLS)
        total_h = jnp.sum(row_total[h], axis=0, keepdims=True)
        qgrad_ref[rows, :] = (
            rowscale_ref[rows, :] * pulls[h]
            - rowpoint_ref[rows, :] * total_h * qt_ref[rows, :].astype(F32)
        )


def attention(gathered, pick, qhi, qlo, qraw, cot, cott, qt, bias, vecs, head_dim):
    quads, owners, rows, features = gathered.shape
    keys = owners * BLOCK
    cols = qhi.shape[1]
    kw, vw = QUAD * HEAD_COLS, QUAD * head_dim
    colscale, colpoint = vecs
    by_col = lambda height, width: pl.BlockSpec((height, width), lambda i, _: (0, i))
    by_row = lambda height, width: pl.BlockSpec((height, width), lambda i, _: (i, 0))
    blocks = pl.BlockSpec(
        (1, owners, rows // BLOCK, BLOCK, features),
        lambda i, _: (i, 0, 0, 0, 0),
        pipeline_mode=pl.Buffered(1 if owners > 16 else 2),
    )
    shape = (quads, owners, rows // BLOCK, BLOCK, features)
    terms, qgrad = pl.pallas_call(
        functools.partial(attention_kernel, head_dim),
        grid_spec=pltpu.PrefetchScalarGridSpec(
            num_scalar_prefetch=1,
            grid=(quads,),
            in_specs=[
                blocks, by_row(kw, cols), by_row(kw, cols),
                by_col(cols, kw), by_col(cols, vw), by_row(vw, cols), by_row(kw, cols),
                pl.BlockSpec(bias.shape, lambda i, _: (0, 0)),
                by_col(1, kw), by_col(1, kw), by_row(kw, 1), by_row(kw, 1),
            ],
            out_specs=[blocks, by_row(kw, cols)],
            scratch_shapes=[
                pltpu.VMEM((QUAD, keys, cols), F32),
                pltpu.VMEM((QUAD, keys, cols), F32),
            ],
        ),
        out_shape=[
            jax.ShapeDtypeStruct(shape, BF16),
            jax.ShapeDtypeStruct((quads * kw, cols), F32),
        ],
        compiler_params=pltpu.CompilerParams(vmem_limit_bytes=60 * 1024 * 1024),
        name="attention",
    )(pick, gathered.reshape(shape), qhi, qlo, qraw, cot, cott, qt, bias, colscale, colpoint,
      colscale.reshape(-1, 1), colpoint.reshape(-1, 1))
    return terms.reshape(gathered.shape), qgrad


def place():
    me = lax.axis_index("res")
    return me, me // 4, (me // 2) % 2, me % 2


def greet(a, depth, side, sibling, me):
    barrier = pltpu.get_barrier_semaphore()

    def signal(target):
        pl.semaphore_signal(
            barrier, inc=1, device_id={"res": target}, device_id_type=pl.DeviceIdType.MESH
        )

    signal(side)
    signal(sibling)
    pl.when(a > 0)(lambda: signal(me - 4))
    pl.when(a < depth - 1)(lambda: signal(me + 4))
    peers = 2 + jnp.where(a > 0, 1, 0) + jnp.where(a < depth - 1, 1, 0)
    pl.semaphore_wait(barrier, peers)


def remote(src, dst, send_sem, recv_sem, target):
    return pltpu.make_async_remote_copy(
        src_ref=src, dst_ref=dst, send_sem=send_sem, recv_sem=recv_sem,
        device_id={"res": target}, device_id_type=pl.DeviceIdType.MESH,
    )


UP, DOWN, SIDE, SIBLING = range(4)


def gather_kernel(depth, x_ref, g_ref, send_sem, recv_sem, local_sem):
    quads = x_ref.shape[0]
    me, a, b, c = place()
    side = me + 2 - 4 * b
    sibling = me + 1 - 2 * c
    targets = {UP: me + 4, DOWN: me - 4, SIDE: side, SIBLING: sibling}
    can = {UP: a < depth - 1, DOWN: a > 0}
    greet(a, depth, side, sibling, me)

    def send(way, slot, q, own=False):
        src = x_ref.at[q] if own else g_ref.at[q, slot]
        return remote(
            src, g_ref.at[q, slot], send_sem.at[way, slot, q], recv_sem.at[slot, q], targets[way]
        )

    def each(fn):
        def body(q, carry):
            fn(q)
            return carry
        lax.fori_loop(0, quads, body, 0)

    def pass_on(ways, slot, q, own=False):
        for way in ways:
            if way in can:
                pl.when(can[way])(lambda way=way: send(way, slot, q, own).start())
            else:
                send(way, slot, q, own).start()

    def settle(ways, slot, q, own=False):
        for way in ways:
            if way in can:
                pl.when(can[way])(lambda way=way: send(way, slot, q, own).wait_send())
            else:
                send(way, slot, q, own).wait_send()

    def arrive(slot, q):
        send(SIBLING, slot, q).wait_recv()

    def own_copy(q):
        return pltpu.make_async_copy(x_ref.at[q], g_ref.at[q, me], local_sem.at[q])

    def start(q):
        pass_on((UP, DOWN, SIDE, SIBLING), me, q, True)
        own_copy(q).start()

    each(start)
    routes = []
    for step in range(1, depth + 1):
        if step < depth:
            routes.append((a - step >= 0, me - 4 * step, (UP, SIDE, SIBLING)))
            routes.append((a + step < depth, me + 4 * step, (DOWN, SIDE, SIBLING)))
        near = step - 1
        routes.append((a - near >= 0, side - 4 * near, (SIBLING,)))
        if near:
            routes.append((a + near < depth, side + 4 * near, (SIBLING,)))

    for valid, slot, ways in routes:
        @pl.when(valid)
        def _(slot=slot, ways=ways):
            def go(q):
                arrive(slot, q)
                pass_on(ways, slot, q)
            each(go)

    def finish(q):
        def body(i, carry):
            arrive(2 * i + 1 - c, q)
            return carry
        lax.fori_loop(0, 2 * depth, body, 0)
        settle((UP, DOWN, SIDE, SIBLING), me, q, True)
        own_copy(q).wait()

    each(finish)
    for valid, slot, ways in routes:
        @pl.when(valid)
        def _(slot=slot, ways=ways):
            each(lambda q: settle(ways, slot, q))


def gather(x, owners):
    quads, rows, features = x.shape
    hbm = pl.BlockSpec(memory_space=pl.ANY)
    return pl.pallas_call(
        functools.partial(gather_kernel, owners // 4),
        in_specs=[hbm],
        out_specs=hbm,
        out_shape=jax.ShapeDtypeStruct((quads, owners, rows, features), x.dtype),
        scratch_shapes=[
            pltpu.SemaphoreType.DMA((4, owners, quads)),
            pltpu.SemaphoreType.DMA((owners, quads)),
            pltpu.SemaphoreType.DMA((quads,)),
        ],
        compiler_params=pltpu.CompilerParams(collective_id=0, has_side_effects=True),
        name="gather_blocks",
    )(x)


def scatter_kernel(
    depth, t_ref, out_ref, acc, from_core, from_side, from_low, from_high,
    local_sem, core_send, core_recv, side_send, side_recv, up_send, low_recv, down_send, high_recv,
):
    quads = t_ref.shape[0]
    me, a, b, c = place()
    side = me + 2 - 4 * b
    sibling = me + 1 - 2 * c
    greet(a, depth, side, sibling, me)

    def own_copy(q, dest):
        return pltpu.make_async_copy(
            t_ref.at[q, 2 * dest + c], acc.at[q, dest], local_sem.at[q, dest]
        )

    def core_copy(q, dest):
        return remote(
            t_ref.at[q, 2 * dest + 1 - c], from_core.at[q, dest],
            core_send.at[q, dest], core_recv.at[q, dest], sibling,
        )

    def side_copy(q, z):
        return remote(
            acc.at[q, 2 * z + 1 - b], from_side.at[q, z], side_send.at[q, z], side_recv.at[q, z], side
        )

    def up_copy(q, z):
        return remote(
            acc.at[q, 2 * z + b], from_low.at[q, z], up_send.at[q, z], low_recv.at[q, z], me + 4
        )

    def down_copy(q, z):
        return remote(
            acc.at[q, 2 * z + b], from_high.at[q, z], down_send.at[q, z], high_recv.at[q, z], me - 4
        )

    def each(fn):
        def body(q, carry):
            fn(q)
            return carry
        lax.fori_loop(0, quads, body, 0)

    def every(fn):
        for step in range(depth - 1, 0, -1):
            pl.when(a + step < depth)(lambda: fn(a + step, 1))
            pl.when(a - step >= 0)(lambda: fn(a - step, -1))
        fn(a, 0)

    def begin(z, _):
        def go(q):
            for lane in (1 - b, b):
                core_copy(q, 2 * z + lane).start()
                own_copy(q, 2 * z + lane).start()
        each(go)

    every(begin)

    def arrived(q, dest):
        own_copy(q, dest).wait()
        core_copy(q, dest).wait_recv()

    def across(z, _):
        def go(q):
            dest = 2 * z + 1 - b
            arrived(q, dest)
            acc[q, dest] = (acc[q, dest].astype(F32) + from_core[q, dest].astype(F32)).astype(BF16)
            side_copy(q, z).start()
        each(go)

    every(across)

    def along(z, way):
        def go(q):
            dest = 2 * z + b
            arrived(q, dest)
            side_copy(q, z).wait_recv()

            def total():
                part = acc[q, dest].astype(F32) + from_core[q, dest].astype(F32)
                return part + from_side[q, z].astype(F32)

            def put(value):
                if way == 0:
                    out_ref[q] = value
                else:
                    acc[q, dest] = value.astype(BF16)

            def below():
                up_copy(q, z).wait_recv()
                return from_low[q, z].astype(F32)

            def above():
                down_copy(q, z).wait_recv()
                return from_high[q, z].astype(F32)

            if way == 1:
                pl.when(a > 0)(lambda: put(total() + below()))
                pl.when(a == 0)(lambda: put(total()))
                up_copy(q, z).start()
            elif way == -1:
                pl.when(a < depth - 1)(lambda: put(total() + above()))
                pl.when(a == depth - 1)(lambda: put(total()))
                down_copy(q, z).start()
            else:
                put(total())

                @pl.when(a > 0)
                def _():
                    out_ref[q] += below()

                @pl.when(a < depth - 1)
                def _():
                    out_ref[q] += above()
        each(go)

    every(along)

    def settle(z, way):
        def go(q):
            for lane in (1 - b, b):
                core_copy(q, 2 * z + lane).wait_send()
            side_copy(q, z).wait_send()
            if way == 1:
                up_copy(q, z).wait_send()
            elif way == -1:
                down_copy(q, z).wait_send()
        each(go)

    every(settle)


def scatter_sum(terms):
    quads, owners, rows, features = terms.shape
    depth = owners // 4
    tile = (rows, features)
    dma = pltpu.SemaphoreType.DMA
    return pl.pallas_call(
        functools.partial(scatter_kernel, depth),
        in_specs=[pl.BlockSpec(memory_space=pl.ANY)],
        out_specs=pl.BlockSpec(memory_space=pltpu.VMEM),
        out_shape=jax.ShapeDtypeStruct((quads, rows, features), F32),
        scratch_shapes=[
            pltpu.VMEM((quads, 2 * depth) + tile, BF16),
            pltpu.VMEM((quads, 2 * depth) + tile, BF16),
            pltpu.VMEM((quads, depth) + tile, BF16),
            pltpu.VMEM((quads, depth) + tile, BF16),
            pltpu.VMEM((quads, depth) + tile, BF16),
        ]
        + [dma((quads, 2 * depth))] * 3
        + [dma((quads, depth))] * 6,
        compiler_params=pltpu.CompilerParams(
            collective_id=1, has_side_effects=True, vmem_limit_bytes=60 * 1024 * 1024
        ),
        name="scatter_sums",
    )(terms)


def split2(x):
    hi = lax.reduce_precision(x, 8, 7)
    return hi.astype(BF16), (x - hi).astype(BF16)


def head_layout(scalars, points, heads, extra):
    rows = scalars.shape[0]
    head_dim = scalars.shape[1] // heads
    count = points.shape[1] // (3 * heads)
    grid = points.reshape(rows, 3, heads, count).transpose(0, 2, 1, 3).reshape(rows, heads, 3 * count)
    pad = jnp.zeros((rows, heads, HEAD_COLS - head_dim - 3 * count - extra.shape[2]), scalars.dtype)
    parts = [scalars.reshape(rows, heads, head_dim), grid, extra, pad]
    return jnp.concatenate(parts, axis=2).reshape(rows, heads * HEAD_COLS)


def prepare(queries, query_points, keys, key_points, weights, out_grad):
    heads = weights.shape[0]
    rows, width = queries.shape
    head_dim = width // heads
    count = query_points.shape[1] // (3 * heads)
    scalar_scale = LOGIT_WEIGHT / math.sqrt(head_dim)
    point_scale = LOGIT_WEIGHT * math.sqrt(2.0 / (9.0 * count)) * weights
    wide = key_points.astype(F32).reshape(rows, 3, heads, count)
    ksq = jnp.sum(wide * wide, axis=(1, 3))
    k1 = lax.reduce_precision(ksq, 8, 7)
    k2 = lax.reduce_precision(ksq - k1, 8, 7)
    k3 = ksq - k1 - k2
    pieces = jnp.stack([k1, k2, k3], axis=2).astype(BF16)
    kx = head_layout(keys, key_points, heads, pieces)
    qraw = head_layout(queries, query_points, heads, jnp.zeros((rows, heads, 3), BF16))
    qt = qraw.T
    slot = jnp.arange(HEAD_COLS)
    is_scalar = slot < head_dim
    is_point = (slot >= head_dim) & (slot < head_dim + 3 * count)
    is_square = (slot >= head_dim + 3 * count) & (slot < head_dim + 3 * count + 3)
    a = point_scale[:, None]
    colscale = jnp.where(is_scalar, scalar_scale, jnp.where(is_point, a, 0.0)).reshape(1, -1)
    colpoint = jnp.where(is_point, a, 0.0).reshape(1, -1)
    square = jnp.where(is_square, -0.5 * a, 0.0).reshape(-1, 1)
    qhi, qlo = split2(qt.astype(F32) * colscale.reshape(-1, 1) + square)
    return kx, qraw, qt, qhi, qlo, out_grad.T, (colscale, colpoint)


def unlayout(x, heads, head_dim, count):
    rows = x.shape[0]
    x = x.reshape(rows, heads, HEAD_COLS)
    points = x[:, :, head_dim : head_dim + 3 * count].reshape(rows, heads, 3, count)
    return (
        x[:, :, :head_dim].reshape(rows, heads * head_dim),
        points.transpose(0, 2, 1, 3).reshape(rows, 3 * heads * count),
    )


def local(
    queries, query_points, keys, key_points, values, point_weights, out_grad,
    fetch_block, key_owner, key_live,
):
    owners = lax.axis_size("res")
    rows, width = queries.shape
    blocks = rows // BLOCK
    heads = point_weights.shape[0]
    head_dim = width // heads
    count = query_points.shape[1] // (3 * heads)
    kx, qraw, qt, qhi, qlo, cott, vecs = prepare(
        queries, query_points, keys, key_points, point_weights, out_grad
    )
    owner_ids = jnp.arange(owners, dtype=jnp.int32)
    named = (key_owner[:, :, None] == owner_ids) & (key_live > 0)[:, :, None]
    live = jnp.any(named, axis=1)
    bias = jnp.repeat(jnp.where(live, 0.0, -jnp.inf).astype(F32).T, BLOCK, axis=1)

    quads = heads // QUAD
    by_quad = [kx.reshape(rows, quads, -1), values.reshape(rows, quads, -1)]
    packed = jnp.concatenate(by_quad, axis=2).transpose(1, 0, 2)
    gathered = gather(packed, owners)
    terms, qgrad = attention(
        gathered, fetch_block[0], qhi, qlo, qraw, out_grad, cott, qt, bias, vecs, head_dim
    )
    summed = scatter_sum(terms).transpose(1, 0, 2)
    query_grad, query_point_grad = unlayout(qgrad.T, heads, head_dim, count)
    split = QUAD * HEAD_COLS
    key_grad, key_point_grad = unlayout(summed[:, :, :split], heads, head_dim, count)
    return query_grad, query_point_grad, key_grad, key_point_grad, summed[:, :, split:].reshape(rows, width)


def solution(mesh):
    rows = P(("grp", "res"), None)
    return jax.shard_map(
        local,
        mesh=mesh,
        in_specs=(rows,) * 5 + (P(),) + (rows,) * 4,
        out_specs=(rows,) * 5,
        check_vma=False,
    )
```

```python
import functools
import math

import jax
import jax.numpy as jnp
from jax import lax
from jax.experimental import pallas as pl
from jax.experimental.pallas import tpu as pltpu
from jax.sharding import PartitionSpec as P

BLOCK = 128
LOGIT_WEIGHT = math.sqrt(1.0 / 3.0)
HEAD_COLS = 64
QUAD = 4
CHUNK = 2 * BLOCK
F32 = jnp.float32
BF16 = jnp.bfloat16


def dot(a, b):
    return jnp.dot(a, b, preferred_element_type=F32)


def fold(x, op):
    return op(x.reshape(x.shape[0] // 8, 8, x.shape[1]), axis=0)


def attention_kernel(
    head_dim, pick_ref, g_ref, qhi_ref, qlo_ref, qraw_ref, cot_ref, cott_ref, qt_ref,
    bias_ref, colscale_ref, colpoint_ref, rowscale_ref, rowpoint_ref,
    term_ref, qgrad_ref, s_ref, d_ref,
):
    keys = s_ref.shape[1]
    wide = QUAD * HEAD_COLS
    cols = qhi_ref.shape[1]
    chunks = keys // CHUNK
    zeros = jnp.zeros((HEAD_COLS, cols), BF16)

    def score_weights(h):
        rows = slice(h * HEAD_COLS, (h + 1) * HEAD_COLS)
        hi, lo = qhi_ref[rows, :], qlo_ref[rows, :]
        parts = [hi, zeros, lo, zeros] if h % 2 == 0 else [zeros, hi, zeros, lo]
        return jnp.concatenate(parts, axis=0)

    def cot_weights(h):
        row = lax.broadcasted_iota(jnp.int32, (QUAD * head_dim, cols), 0)
        keep = (row >= h * head_dim) & (row < (h + 1) * head_dim)
        return jnp.where(keep, cott_ref[...], jnp.zeros((), BF16))

    def load(i, span):
        first = g_ref[0, 2 * i, pick_ref[2 * i], :, span]
        second = g_ref[0, 2 * i + 1, pick_ref[2 * i + 1], :, span]
        return jnp.concatenate([first, second], axis=0)

    def store(i, span, value):
        for j in range(2):
            o = 2 * i + j
            part = value[j * BLOCK : (j + 1) * BLOCK].astype(BF16)
            term_ref[0, o, pick_ref[o], :, span] = part
            term_ref[0, o, 1 - pick_ref[o], :, span] = jnp.zeros_like(part)

    qw = [score_weights(h) for h in range(QUAD)]
    ow = [cot_weights(h) for h in range(QUAD)]

    def scores(i, highest):
        rows = pl.ds(pl.multiple_of(i * CHUNK, CHUNK), CHUNK)
        low = bias_ref[pl.ds(i * 2, 1), :]
        high = bias_ref[pl.ds(i * 2 + 1, 1), :]
        vals = load(i, slice(wide, wide + 128))
        out = []
        for h in range(QUAD):
            pair = load(i, slice((h // 2) * 128, (h // 2 + 1) * 128))
            s = dot(jnp.concatenate([pair, pair], axis=1), qw[h])
            s = jnp.concatenate([s[:BLOCK] + low, s[BLOCK:] + high], axis=0)
            s_ref[h, rows, :] = s
            out.append(jnp.maximum(highest[h], fold(s, jnp.max)))
            d_ref[h, rows, :] = dot(vals, ow[h])
        return tuple(out)

    highest = lax.fori_loop(
        0, chunks, scores, tuple(jnp.full((8, cols), -jnp.inf, F32) for _ in range(QUAD))
    )
    highest = [jnp.max(x, axis=0, keepdims=True) for x in highest]

    def exps(i, total):
        rows = pl.ds(pl.multiple_of(i * CHUNK, CHUNK), CHUNK)
        out = []
        for h in range(QUAD):
            e = jnp.exp(s_ref[h, rows, :] - highest[h])
            s_ref[h, rows, :] = e
            out.append(total[h] + fold(e, jnp.sum))
        return tuple(out)

    zero8 = tuple(jnp.zeros((8, cols), F32) for _ in range(QUAD))
    total = lax.fori_loop(0, chunks, exps, zero8)
    inverse = [1.0 / jnp.sum(x, axis=0, keepdims=True) for x in total]

    def deltas(i, delta):
        rows = pl.ds(pl.multiple_of(i * CHUNK, CHUNK), CHUNK)
        out = []
        for h in range(QUAD):
            p = s_ref[h, rows, :] * inverse[h]
            low = p.astype(BF16).astype(F32)
            out.append(delta[h] + fold(low * d_ref[h, rows, :], jnp.sum))
        return tuple(out)

    delta = lax.fori_loop(0, chunks, deltas, zero8)
    delta = [jnp.sum(x, axis=0, keepdims=True) for x in delta]

    lane = lax.broadcasted_iota(jnp.int32, (cols, 128), 1)
    qk = []
    ok = []
    for h in range(QUAD):
        pair = qraw_ref[:, (h // 2) * 128 : (h // 2 + 1) * 128]
        qk.append(jnp.where(lane // HEAD_COLS == h % 2, pair, jnp.zeros((), BF16)))
        ok.append(jnp.where(lane // head_dim == h, cot_ref[...], jnp.zeros((), BF16)))
    half = lax.broadcasted_iota(jnp.int32, (CHUNK, 128), 1) < HEAD_COLS

    def grads(i, carry):
        row_total, pulls = carry
        rows = pl.ds(pl.multiple_of(i * CHUNK, CHUNK), CHUNK)
        new_total, new_pulls = [], []
        vterm = None
        for g in range(QUAD // 2):
            pair = load(i, slice(g * 128, (g + 1) * 128))
            kterm = None
            col_totals = []
            for h in (2 * g, 2 * g + 1):
                p = s_ref[h, rows, :] * inverse[h]
                p_low = p.astype(BF16)
                ds = p * (d_ref[h, rows, :] - delta[h])
                ds_low = ds.astype(BF16)
                new_total.append(row_total[h] + fold(ds, jnp.sum))
                col_totals.append(jnp.sum(ds, axis=1, keepdims=True))
                kt = dot(ds_low, qk[h])
                kterm = kt if kterm is None else kterm + kt
                vt = dot(p_low, ok[h])
                vterm = vt if vterm is None else vterm + vt
                pull = lax.dot_general(
                    pair, ds_low, (((0,), (0,)), ((), ())), preferred_element_type=F32
                )
                off = (h % 2) * HEAD_COLS
                new_pulls.append(pulls[h] + pull[off : off + HEAD_COLS])
            sums = jnp.where(half, col_totals[0], col_totals[1])
            span = slice(g * 128, (g + 1) * 128)
            kterm = colscale_ref[:, span] * kterm - colpoint_ref[:, span] * sums * pair.astype(F32)
            store(i, span, kterm)
        store(i, slice(wide, wide + 128), vterm)
        return tuple(new_total), tuple(new_pulls)

    pull0 = tuple(jnp.zeros((HEAD_COLS, cols), F32) for _ in range(QUAD))
    row_total, pulls = lax.fori_loop(0, chunks, grads, (zero8, pull0))
    for h in range(QUAD):
        rows = slice(h * HEAD_COLS, (h + 1) * HEAD_COLS)
        total_h = jnp.sum(row_total[h], axis=0, keepdims=True)
        qgrad_ref[rows, :] = (
            rowscale_ref[rows, :] * pulls[h]
            - rowpoint_ref[rows, :] * total_h * qt_ref[rows, :].astype(F32)
        )


def attention(gathered, pick, qhi, qlo, qraw, cot, cott, qt, bias, vecs, head_dim):
    quads, owners, rows, features = gathered.shape
    keys = owners * BLOCK
    cols = qhi.shape[1]
    kw, vw = QUAD * HEAD_COLS, QUAD * head_dim
    colscale, colpoint = vecs
    by_col = lambda height, width: pl.BlockSpec((height, width), lambda i, _: (0, i))
    by_row = lambda height, width: pl.BlockSpec((height, width), lambda i, _: (i, 0))
    blocks = pl.BlockSpec(
        (1, owners, rows // BLOCK, BLOCK, features),
        lambda i, _: (i, 0, 0, 0, 0),
        pipeline_mode=pl.Buffered(1 if owners > 16 else 2),
    )
    shape = (quads, owners, rows // BLOCK, BLOCK, features)
    terms, qgrad = pl.pallas_call(
        functools.partial(attention_kernel, head_dim),
        grid_spec=pltpu.PrefetchScalarGridSpec(
            num_scalar_prefetch=1,
            grid=(quads,),
            in_specs=[
                blocks, by_row(kw, cols), by_row(kw, cols),
                by_col(cols, kw), by_col(cols, vw), by_row(vw, cols), by_row(kw, cols),
                pl.BlockSpec(bias.shape, lambda i, _: (0, 0)),
                by_col(1, kw), by_col(1, kw), by_row(kw, 1), by_row(kw, 1),
            ],
            out_specs=[blocks, by_row(kw, cols)],
            scratch_shapes=[
                pltpu.VMEM((QUAD, keys, cols), F32),
                pltpu.VMEM((QUAD, keys, cols), F32),
            ],
        ),
        out_shape=[
            jax.ShapeDtypeStruct(shape, BF16),
            jax.ShapeDtypeStruct((quads * kw, cols), F32),
        ],
        compiler_params=pltpu.CompilerParams(vmem_limit_bytes=60 * 1024 * 1024),
        name="attention",
    )(pick, gathered.reshape(shape), qhi, qlo, qraw, cot, cott, qt, bias, colscale, colpoint,
      colscale.reshape(-1, 1), colpoint.reshape(-1, 1))
    return terms.reshape(gathered.shape), qgrad


def place():
    me = lax.axis_index("res")
    return me, me // 4, (me // 2) % 2, me % 2


def greet(a, depth, side, sibling, me):
    barrier = pltpu.get_barrier_semaphore()

    def signal(target):
        pl.semaphore_signal(
            barrier, inc=1, device_id={"res": target}, device_id_type=pl.DeviceIdType.MESH
        )

    signal(side)
    signal(sibling)
    pl.when(a > 0)(lambda: signal(me - 4))
    pl.when(a < depth - 1)(lambda: signal(me + 4))
    peers = 2 + jnp.where(a > 0, 1, 0) + jnp.where(a < depth - 1, 1, 0)
    pl.semaphore_wait(barrier, peers)


def remote(src, dst, send_sem, recv_sem, target):
    return pltpu.make_async_remote_copy(
        src_ref=src, dst_ref=dst, send_sem=send_sem, recv_sem=recv_sem,
        device_id={"res": target}, device_id_type=pl.DeviceIdType.MESH,
    )


UP, DOWN, SIDE, SIBLING = range(4)


def gather_kernel(depth, x_ref, g_ref, send_sem, recv_sem, local_sem):
    quads = x_ref.shape[0]
    me, a, b, c = place()
    side = me + 2 - 4 * b
    sibling = me + 1 - 2 * c
    targets = {UP: me + 4, DOWN: me - 4, SIDE: side, SIBLING: sibling}
    can = {UP: a < depth - 1, DOWN: a > 0}
    greet(a, depth, side, sibling, me)

    def send(way, slot, q, own=False):
        src = x_ref.at[q] if own else g_ref.at[q, slot]
        return remote(
            src, g_ref.at[q, slot], send_sem.at[way, slot, q], recv_sem.at[slot, q], targets[way]
        )

    def each(fn):
        def body(q, carry):
            fn(q)
            return carry
        lax.fori_loop(0, quads, body, 0)

    def pass_on(ways, slot, q, own=False):
        for way in ways:
            if way in can:
                pl.when(can[way])(lambda way=way: send(way, slot, q, own).start())
            else:
                send(way, slot, q, own).start()

    def settle(ways, slot, q, own=False):
        for way in ways:
            if way in can:
                pl.when(can[way])(lambda way=way: send(way, slot, q, own).wait_send())
            else:
                send(way, slot, q, own).wait_send()

    def arrive(slot, q):
        send(SIBLING, slot, q).wait_recv()

    def own_copy(q):
        return pltpu.make_async_copy(x_ref.at[q], g_ref.at[q, me], local_sem.at[q])

    def start(q):
        pass_on((UP, DOWN, SIDE, SIBLING), me, q, True)
        own_copy(q).start()

    each(start)
    routes = []
    for step in range(1, depth + 1):
        if step < depth:
            routes.append((a - step >= 0, me - 4 * step, (UP, SIDE, SIBLING)))
            routes.append((a + step < depth, me + 4 * step, (DOWN, SIDE, SIBLING)))
        near = step - 1
        routes.append((a - near >= 0, side - 4 * near, (SIBLING,)))
        if near:
            routes.append((a + near < depth, side + 4 * near, (SIBLING,)))

    for valid, slot, ways in routes:
        @pl.when(valid)
        def _(slot=slot, ways=ways):
            def go(q):
                arrive(slot, q)
                pass_on(ways, slot, q)
            each(go)

    def finish(q):
        def body(i, carry):
            arrive(2 * i + 1 - c, q)
            return carry
        lax.fori_loop(0, 2 * depth, body, 0)
        settle((UP, DOWN, SIDE, SIBLING), me, q, True)
        own_copy(q).wait()

    each(finish)
    for valid, slot, ways in routes:
        @pl.when(valid)
        def _(slot=slot, ways=ways):
            each(lambda q: settle(ways, slot, q))


def gather(x, owners):
    quads, rows, features = x.shape
    hbm = pl.BlockSpec(memory_space=pl.ANY)
    return pl.pallas_call(
        functools.partial(gather_kernel, owners // 4),
        in_specs=[hbm],
        out_specs=hbm,
        out_shape=jax.ShapeDtypeStruct((quads, owners, rows, features), x.dtype),
        scratch_shapes=[
            pltpu.SemaphoreType.DMA((4, owners, quads)),
            pltpu.SemaphoreType.DMA((owners, quads)),
            pltpu.SemaphoreType.DMA((quads,)),
        ],
        compiler_params=pltpu.CompilerParams(collective_id=0, has_side_effects=True),
        name="gather_blocks",
    )(x)


def scatter_kernel(
    depth, t_ref, out_ref, acc, from_core, from_side, from_low, from_high,
    local_sem, core_send, core_recv, side_send, side_recv, up_send, low_recv, down_send, high_recv,
):
    quads = t_ref.shape[0]
    me, a, b, c = place()
    side = me + 2 - 4 * b
    sibling = me + 1 - 2 * c
    greet(a, depth, side, sibling, me)

    def own_copy(q, dest):
        return pltpu.make_async_copy(
            t_ref.at[q, 2 * dest + c], acc.at[q, dest], local_sem.at[q, dest]
        )

    def core_copy(q, dest):
        return remote(
            t_ref.at[q, 2 * dest + 1 - c], from_core.at[q, dest],
            core_send.at[q, dest], core_recv.at[q, dest], sibling,
        )

    def side_copy(q, z):
        return remote(
            acc.at[q, 2 * z + 1 - b], from_side.at[q, z], side_send.at[q, z], side_recv.at[q, z], side
        )

    def up_copy(q, z):
        return remote(
            acc.at[q, 2 * z + b], from_low.at[q, z], up_send.at[q, z], low_recv.at[q, z], me + 4
        )

    def down_copy(q, z):
        return remote(
            acc.at[q, 2 * z + b], from_high.at[q, z], down_send.at[q, z], high_recv.at[q, z], me - 4
        )

    def each(fn):
        def body(q, carry):
            fn(q)
            return carry
        lax.fori_loop(0, quads, body, 0)

    def every(fn):
        for step in range(depth - 1, 0, -1):
            pl.when(a + step < depth)(lambda: fn(a + step, 1))
            pl.when(a - step >= 0)(lambda: fn(a - step, -1))
        fn(a, 0)

    def begin(z, _):
        def go(q):
            for lane in (1 - b, b):
                core_copy(q, 2 * z + lane).start()
                own_copy(q, 2 * z + lane).start()
        each(go)

    every(begin)

    def arrived(q, dest):
        own_copy(q, dest).wait()
        core_copy(q, dest).wait_recv()

    def across(z, _):
        def go(q):
            dest = 2 * z + 1 - b
            arrived(q, dest)
            acc[q, dest] = (acc[q, dest].astype(F32) + from_core[q, dest].astype(F32)).astype(BF16)
            side_copy(q, z).start()
        each(go)

    every(across)

    def along(z, way):
        def go(q):
            dest = 2 * z + b
            arrived(q, dest)
            side_copy(q, z).wait_recv()

            def total():
                part = acc[q, dest].astype(F32) + from_core[q, dest].astype(F32)
                return part + from_side[q, z].astype(F32)

            def put(value):
                if way == 0:
                    out_ref[q] = value
                else:
                    acc[q, dest] = value.astype(BF16)

            def below():
                up_copy(q, z).wait_recv()
                return from_low[q, z].astype(F32)

            def above():
                down_copy(q, z).wait_recv()
                return from_high[q, z].astype(F32)

            if way == 1:
                pl.when(a > 0)(lambda: put(total() + below()))
                pl.when(a == 0)(lambda: put(total()))
                up_copy(q, z).start()
            elif way == -1:
                pl.when(a < depth - 1)(lambda: put(total() + above()))
                pl.when(a == depth - 1)(lambda: put(total()))
                down_copy(q, z).start()
            else:
                put(total())

                @pl.when(a > 0)
                def _():
                    out_ref[q] += below()

                @pl.when(a < depth - 1)
                def _():
                    out_ref[q] += above()
        each(go)

    every(along)

    def settle(z, way):
        def go(q):
            for lane in (1 - b, b):
                core_copy(q, 2 * z + lane).wait_send()
            side_copy(q, z).wait_send()
            if way == 1:
                up_copy(q, z).wait_send()
            elif way == -1:
                down_copy(q, z).wait_send()
        each(go)

    every(settle)


def scatter_sum(terms):
    quads, owners, rows, features = terms.shape
    depth = owners // 4
    tile = (rows, features)
    dma = pltpu.SemaphoreType.DMA
    return pl.pallas_call(
        functools.partial(scatter_kernel, depth),
        in_specs=[pl.BlockSpec(memory_space=pl.ANY)],
        out_specs=pl.BlockSpec(memory_space=pltpu.VMEM),
        out_shape=jax.ShapeDtypeStruct((quads, rows, features), F32),
        scratch_shapes=[
            pltpu.VMEM((quads, 2 * depth) + tile, BF16),
            pltpu.VMEM((quads, 2 * depth) + tile, BF16),
            pltpu.VMEM((quads, depth) + tile, BF16),
            pltpu.VMEM((quads, depth) + tile, BF16),
            pltpu.VMEM((quads, depth) + tile, BF16),
        ]
        + [dma((quads, 2 * depth))] * 3
        + [dma((quads, depth))] * 6,
        compiler_params=pltpu.CompilerParams(
            collective_id=1, has_side_effects=True, vmem_limit_bytes=60 * 1024 * 1024
        ),
        name="scatter_sums",
    )(terms)


def fused_kernel(
    depth, head_dim, x_ref, pick_ref, qhi_ref, qlo_ref, qraw_ref, cot_ref, cott_ref, bias_ref,
    colscale_ref, colpoint_ref, out_ref, pull_ref, rowsum_ref,
    g, terms, from_core, from_side, from_low, from_high, s_ref, d_ref,
    send_sem, recv_sem, local_sem,
    core_send, core_recv, side_send, side_recv, up_send, low_recv, down_send, high_recv,
):
    quads = x_ref.shape[0]
    cols = qhi_ref.shape[2]
    chunks = 2 * depth
    wide = QUAD * HEAD_COLS
    me, a, b, c = place()
    side = me + 2 - 4 * b
    sibling = me + 1 - 2 * c
    targets = {UP: me + 4, DOWN: me - 4, SIDE: side, SIBLING: sibling}
    can = {UP: a < depth - 1, DOWN: a > 0}
    every_way = (UP, DOWN, SIDE, SIBLING)
    greet(a, depth, side, sibling, me)

    def send(way, slot, q, own=False):
        src = x_ref.at[q] if own else g.at[q, slot]
        return remote(
            src, g.at[q, slot], send_sem.at[way, slot, q], recv_sem.at[slot, q], targets[way]
        )

    def act(ways, slot, q, own, fn):
        for way in ways:
            if way in can:
                pl.when(can[way])(lambda way=way: fn(send(way, slot, q, own)))
            else:
                fn(send(way, slot, q, own))

    def own_copy(q):
        return pltpu.make_async_copy(x_ref.at[q], g.at[q, me], local_sem.at[q])

    def gather_own(q):
        act(every_way, me, q, True, lambda copy: copy.start())
        own_copy(q).start()

    levels = []
    for step in range(1, depth + 1):
        routes = []
        if step < depth:
            routes.append((a - step >= 0, me - 4 * step, (UP, SIDE, SIBLING)))
            routes.append((a + step < depth, me + 4 * step, (DOWN, SIDE, SIBLING)))
        near = step - 1
        routes.append((a - near >= 0, side - 4 * near, (SIBLING,)))
        if near:
            routes.append((a + near < depth, side + 4 * near, (SIBLING,)))
        levels.append(routes)

    def gather_level(step, q):
        for valid, slot, ways in levels[step - 1]:
            @pl.when(valid)
            def _(slot=slot, ways=ways):
                send(SIBLING, slot, q).wait_recv()
                act(ways, slot, q, False, lambda copy: copy.start())

    def gather_finish(q):
        def body(i, carry):
            send(SIBLING, 2 * i + 1 - c, q).wait_recv()
            return carry
        lax.fori_loop(0, 2 * depth, body, 0)
        own_copy(q).wait()

    def gather_settle(q):
        act(every_way, me, q, True, lambda copy: copy.wait_send())
        for routes in levels:
            for valid, slot, ways in routes:
                @pl.when(valid)
                def _(slot=slot, ways=ways):
                    act(ways, slot, q, False, lambda copy: copy.wait_send())

    def core_copy(q, dest):
        return remote(
            terms.at[q, 1 - c, dest], from_core.at[q, dest],
            core_send.at[q, dest], core_recv.at[q, dest], sibling,
        )

    def side_copy(q, z):
        return remote(
            terms.at[q, c, 2 * z + 1 - b], from_side.at[q, z],
            side_send.at[q, z], side_recv.at[q, z], side,
        )

    def up_copy(q, z):
        return remote(
            terms.at[q, c, 2 * z + b], from_low.at[q, z], up_send.at[q, z], low_recv.at[q, z], me + 4
        )

    def down_copy(q, z):
        return remote(
            terms.at[q, c, 2 * z + b], from_high.at[q, z],
            down_send.at[q, z], high_recv.at[q, z], me - 4,
        )

    def at_step(step, fn):
        if step == 0:
            fn(a, 0)
        else:
            pl.when(a + step < depth)(lambda: fn(a + step, 1))
            pl.when(a - step >= 0)(lambda: fn(a - step, -1))

    def every(fn):
        for step in range(depth - 1, -1, -1):
            at_step(step, fn)

    def sum_begin(q):
        def go(z, _):
            core_copy(q, 2 * z + 1 - b).start()
            core_copy(q, 2 * z + b).start()
        every(go)

    def sum_across(q):
        def go(z, _):
            dest = 2 * z + 1 - b
            core_copy(q, dest).wait_recv()
            total = terms[q, c, dest].astype(F32) + from_core[q, dest].astype(F32)
            terms[q, c, dest] = total.astype(BF16)
            side_copy(q, z).start()
        every(go)

    def sum_along(step, q):
        def go(z, way):
            dest = 2 * z + b
            core_copy(q, dest).wait_recv()
            side_copy(q, z).wait_recv()

            def total():
                part = terms[q, c, dest].astype(F32) + from_core[q, dest].astype(F32)
                return part + from_side[q, z].astype(F32)

            def put(value):
                terms[q, c, dest] = value.astype(BF16)

            def below():
                up_copy(q, z).wait_recv()
                return from_low[q, z].astype(F32)

            def above():
                down_copy(q, z).wait_recv()
                return from_high[q, z].astype(F32)

            if way == 1:
                pl.when(a > 0)(lambda: put(total() + below()))
                pl.when(a == 0)(lambda: put(total()))
                up_copy(q, z).start()
            elif way == -1:
                pl.when(a < depth - 1)(lambda: put(total() + above()))
                pl.when(a == depth - 1)(lambda: put(total()))
                down_copy(q, z).start()
            else:
                out_ref[q] = total()

                @pl.when(a > 0)
                def _():
                    out_ref[q] += below()

                @pl.when(a < depth - 1)
                def _():
                    out_ref[q] += above()
        at_step(step, go)

    def sum_settle(q):
        def go(z, way):
            core_copy(q, 2 * z + 1 - b).wait_send()
            core_copy(q, 2 * z + b).wait_send()
            side_copy(q, z).wait_send()
            if way == 1:
                up_copy(q, z).wait_send()
            elif way == -1:
                down_copy(q, z).wait_send()
        every(go)

    zeros = jnp.zeros((HEAD_COLS, cols), BF16)
    zero8 = tuple(jnp.zeros((8, cols), F32) for _ in range(QUAD))
    lane = lax.broadcasted_iota(jnp.int32, (cols, 128), 1)
    half = lax.broadcasted_iota(jnp.int32, (CHUNK, 128), 1) < HEAD_COLS

    def quad_step(q, carry0):
        ahead = lambda fn: pl.when(q + 1 < quads)(fn)
        behind = lambda fn: pl.when(q > 0)(fn)

        def load(i, span):
            parts = []
            for j in range(2):
                o = 2 * i + j
                w = jnp.broadcast_to(pick_ref[pl.ds(o, 1), :], (BLOCK, 128)).astype(BF16)
                low, high = g[q, o, :BLOCK, span], g[q, o, BLOCK:, span]
                parts.append(low * (1 - w) + high * w)
            return jnp.concatenate(parts, axis=0)

        def store(i, span, value):
            for j in range(2):
                w = jnp.broadcast_to(pick_ref[pl.ds(2 * i + j, 1), :], (BLOCK, 128))
                part = value[j * BLOCK : (j + 1) * BLOCK]
                terms[q, j, i, :BLOCK, span] = (part * (1.0 - w)).astype(BF16)
                terms[q, j, i, BLOCK:, span] = (part * w).astype(BF16)

        def score_weights(h):
            rows = slice(h * HEAD_COLS, (h + 1) * HEAD_COLS)
            hi, lo = qhi_ref[q, rows, :], qlo_ref[q, rows, :]
            parts = [hi, zeros, lo, zeros] if h % 2 == 0 else [zeros, hi, zeros, lo]
            return jnp.concatenate(parts, axis=0)

        def cot_weights(h):
            row = lax.broadcasted_iota(jnp.int32, (QUAD * head_dim, cols), 0)
            keep = (row >= h * head_dim) & (row < (h + 1) * head_dim)
            return jnp.where(keep, cott_ref[q], jnp.zeros((), BF16))

        behind(lambda: sum_begin(q - 1))
        ahead(lambda: gather_level(1, q + 1))
        qw = [score_weights(h) for h in range(QUAD)]
        ow = [cot_weights(h) for h in range(QUAD)]

        def scores(i, highest):
            rows = pl.ds(pl.multiple_of(i * CHUNK, CHUNK), CHUNK)
            low = bias_ref[pl.ds(i * 2, 1), :]
            high = bias_ref[pl.ds(i * 2 + 1, 1), :]
            vals = load(i, slice(wide, wide + 128))
            pairs = [load(i, slice(n * 128, (n + 1) * 128)) for n in range(QUAD // 2)]
            out = []
            for h in range(QUAD):
                pair = pairs[h // 2]
                s = dot(jnp.concatenate([pair, pair], axis=1), qw[h])
                s = jnp.concatenate([s[:BLOCK] + low, s[BLOCK:] + high], axis=0)
                s_ref[h, rows, :] = s
                out.append(jnp.maximum(highest[h], fold(s, jnp.max)))
                d_ref[h, rows, :] = dot(vals, ow[h])
            return tuple(out)

        highest = lax.fori_loop(
            0, chunks, scores, tuple(jnp.full((8, cols), -jnp.inf, F32) for _ in range(QUAD))
        )
        highest = [jnp.max(x, axis=0, keepdims=True) for x in highest]
        behind(lambda: sum_across(q - 1))
        ahead(lambda: gather_level(2, q + 1))

        def exps(i, total):
            rows = pl.ds(pl.multiple_of(i * CHUNK, CHUNK), CHUNK)
            out = []
            for h in range(QUAD):
                e = jnp.exp(s_ref[h, rows, :] - highest[h])
                s_ref[h, rows, :] = e
                out.append(total[h] + fold(e, jnp.sum))
            return tuple(out)

        total = lax.fori_loop(0, chunks, exps, zero8)
        inverse = [1.0 / jnp.sum(x, axis=0, keepdims=True) for x in total]
        ahead(lambda: gather_level(3, q + 1))
        pl.when(q + 2 < quads)(lambda: gather_own(q + 2))
        behind(lambda: sum_along(depth - 1, q - 1))

        def deltas(i, delta):
            rows = pl.ds(pl.multiple_of(i * CHUNK, CHUNK), CHUNK)
            out = []
            for h in range(QUAD):
                p = s_ref[h, rows, :] * inverse[h]
                low = p.astype(BF16).astype(F32)
                out.append(delta[h] + fold(low * d_ref[h, rows, :], jnp.sum))
            return tuple(out)

        delta = lax.fori_loop(0, chunks, deltas, zero8)
        delta = [jnp.sum(x, axis=0, keepdims=True) for x in delta]
        for step in range(4, depth + 1):
            ahead(lambda step=step: gather_level(step, q + 1))
        behind(lambda: sum_along(depth - 2, q - 1))

        qk = []
        ok = []
        for h in range(QUAD):
            pair = qraw_ref[q, :, (h // 2) * 128 : (h // 2 + 1) * 128]
            qk.append(jnp.where(lane // HEAD_COLS == h % 2, pair, jnp.zeros((), BF16)))
            ok.append(jnp.where(lane // head_dim == h, cot_ref[q], jnp.zeros((), BF16)))

        def grads(i, carry):
            row_total, pulls = carry
            rows = pl.ds(pl.multiple_of(i * CHUNK, CHUNK), CHUNK)
            new_total, new_pulls = [], []
            vterm = None
            for n in range(QUAD // 2):
                span = slice(n * 128, (n + 1) * 128)
                pair = load(i, span)
                kterm = None
                col_totals = []
                for h in (2 * n, 2 * n + 1):
                    p = s_ref[h, rows, :] * inverse[h]
                    p_low = p.astype(BF16)
                    ds = p * (d_ref[h, rows, :] - delta[h])
                    ds_low = ds.astype(BF16)
                    new_total.append(row_total[h] + fold(ds, jnp.sum))
                    col_totals.append(jnp.sum(ds, axis=1, keepdims=True))
                    kt = dot(ds_low, qk[h])
                    kterm = kt if kterm is None else kterm + kt
                    vt = dot(p_low, ok[h])
                    vterm = vt if vterm is None else vterm + vt
                    pull = lax.dot_general(
                        pair, ds_low, (((0,), (0,)), ((), ())), preferred_element_type=F32
                    )
                    off = (h % 2) * HEAD_COLS
                    new_pulls.append(pulls[h] + pull[off : off + HEAD_COLS])
                sums = jnp.where(half, col_totals[0], col_totals[1])
                kterm = (
                    colscale_ref[q, :, span] * kterm
                    - colpoint_ref[q, :, span] * sums * pair.astype(F32)
                )
                store(i, span, kterm)
            store(i, slice(wide, wide + 128), vterm)
            return tuple(new_total), tuple(new_pulls)

        pull0 = tuple(jnp.zeros((HEAD_COLS, cols), F32) for _ in range(QUAD))
        row_total, pulls = lax.fori_loop(0, chunks, grads, (zero8, pull0))
        for h in range(QUAD):
            pull_ref[q, h * HEAD_COLS : (h + 1) * HEAD_COLS, :] = pulls[h]
            rowsum_ref[q, h * 8 : (h + 1) * 8, :] = row_total[h]
        for step in range(depth - 3, -1, -1):
            behind(lambda step=step: sum_along(step, q - 1))
        ahead(lambda: gather_finish(q + 1))
        return carry0

    gather_own(0)
    gather_own(1)
    for step in range(1, depth + 1):
        gather_level(step, 0)
    gather_finish(0)
    lax.fori_loop(0, quads, quad_step, 0)
    last = quads - 1
    sum_begin(last)
    sum_across(last)
    for step in range(depth - 1, -1, -1):
        sum_along(step, last)

    def settle(q, carry):
        gather_settle(q)
        sum_settle(q)
        return carry

    lax.fori_loop(0, quads, settle, 0)


def fused(packed, owners, pick, qhi, qlo, qraw, cot, cott, bias, vecs, head_dim):
    quads, rows, features = packed.shape
    depth = owners // 4
    cols = qhi.shape[1]
    kw, vw = QUAD * HEAD_COLS, QUAD * head_dim
    by_cols = lambda x, width: x.reshape(x.shape[0], quads, width).transpose(1, 0, 2)
    by_rows = lambda x, height: x.reshape(quads, height, x.shape[1])
    tile = (rows, features)
    dma = pltpu.SemaphoreType.DMA
    vmem = pl.BlockSpec(memory_space=pltpu.VMEM)
    weights = jnp.broadcast_to(pick.astype(F32)[:, None], (owners, 128))
    return pl.pallas_call(
        functools.partial(fused_kernel, depth, head_dim),
        in_specs=[pl.BlockSpec(memory_space=pl.ANY)] + [vmem] * 9,
        out_specs=[vmem] * 3,
        out_shape=[
            jax.ShapeDtypeStruct((quads,) + tile, F32),
            jax.ShapeDtypeStruct((quads, kw, cols), F32),
            jax.ShapeDtypeStruct((quads, QUAD * 8, cols), F32),
        ],
        scratch_shapes=[
            pltpu.VMEM((quads, owners) + tile, BF16),
            pltpu.VMEM((quads, 2, 2 * depth) + tile, BF16),
            pltpu.VMEM((quads, 2 * depth) + tile, BF16),
            pltpu.VMEM((quads, depth) + tile, BF16),
            pltpu.VMEM((quads, depth) + tile, BF16),
            pltpu.VMEM((quads, depth) + tile, BF16),
            pltpu.VMEM((QUAD, owners * BLOCK, cols), F32),
            pltpu.VMEM((QUAD, owners * BLOCK, cols), F32),
            dma((4, owners, quads)), dma((owners, quads)), dma((quads,)),
        ]
        + [dma((quads, 2 * depth))] * 2
        + [dma((quads, depth))] * 6,
        compiler_params=pltpu.CompilerParams(
            collective_id=2, has_side_effects=True, vmem_limit_bytes=63 * 1024 * 1024
        ),
        name="fused_attention",
    )(packed, weights, by_rows(qhi, kw), by_rows(qlo, kw), by_cols(qraw, kw), by_cols(cot, vw),
      by_rows(cott, vw), bias, by_cols(vecs[0], kw), by_cols(vecs[1], kw))


def split2(x):
    hi = lax.reduce_precision(x, 8, 7)
    return hi.astype(BF16), (x - hi).astype(BF16)


def head_layout(scalars, points, heads, extra):
    rows = scalars.shape[0]
    head_dim = scalars.shape[1] // heads
    count = points.shape[1] // (3 * heads)
    grid = points.reshape(rows, 3, heads, count).transpose(0, 2, 1, 3).reshape(rows, heads, 3 * count)
    pad = jnp.zeros((rows, heads, HEAD_COLS - head_dim - 3 * count - extra.shape[2]), scalars.dtype)
    parts = [scalars.reshape(rows, heads, head_dim), grid, extra, pad]
    return jnp.concatenate(parts, axis=2).reshape(rows, heads * HEAD_COLS)


def prepare(queries, query_points, keys, key_points, weights, out_grad):
    heads = weights.shape[0]
    rows, width = queries.shape
    head_dim = width // heads
    count = query_points.shape[1] // (3 * heads)
    scalar_scale = LOGIT_WEIGHT / math.sqrt(head_dim)
    point_scale = LOGIT_WEIGHT * math.sqrt(2.0 / (9.0 * count)) * weights
    wide = key_points.astype(F32).reshape(rows, 3, heads, count)
    ksq = jnp.sum(wide * wide, axis=(1, 3))
    k1 = lax.reduce_precision(ksq, 8, 7)
    k2 = lax.reduce_precision(ksq - k1, 8, 7)
    k3 = ksq - k1 - k2
    pieces = jnp.stack([k1, k2, k3], axis=2).astype(BF16)
    kx = head_layout(keys, key_points, heads, pieces)
    qraw = head_layout(queries, query_points, heads, jnp.zeros((rows, heads, 3), BF16))
    qt = qraw.T
    slot = jnp.arange(HEAD_COLS)
    is_scalar = slot < head_dim
    is_point = (slot >= head_dim) & (slot < head_dim + 3 * count)
    is_square = (slot >= head_dim + 3 * count) & (slot < head_dim + 3 * count + 3)
    a = point_scale[:, None]
    colscale = jnp.where(is_scalar, scalar_scale, jnp.where(is_point, a, 0.0)).reshape(1, -1)
    colpoint = jnp.where(is_point, a, 0.0).reshape(1, -1)
    square = jnp.where(is_square, -0.5 * a, 0.0).reshape(-1, 1)
    qhi, qlo = split2(qt.astype(F32) * colscale.reshape(-1, 1) + square)
    return kx, qraw, qt, qhi, qlo, out_grad.T, (colscale, colpoint)


def unlayout(x, heads, head_dim, count):
    rows = x.shape[0]
    x = x.reshape(rows, heads, HEAD_COLS)
    points = x[:, :, head_dim : head_dim + 3 * count].reshape(rows, heads, 3, count)
    return (
        x[:, :, :head_dim].reshape(rows, heads * head_dim),
        points.transpose(0, 2, 1, 3).reshape(rows, 3 * heads * count),
    )


def local(
    queries, query_points, keys, key_points, values, point_weights, out_grad,
    fetch_block, key_owner, key_live,
):
    owners = lax.axis_size("res")
    rows, width = queries.shape
    blocks = rows // BLOCK
    heads = point_weights.shape[0]
    head_dim = width // heads
    count = query_points.shape[1] // (3 * heads)
    kx, qraw, qt, qhi, qlo, cott, vecs = prepare(
        queries, query_points, keys, key_points, point_weights, out_grad
    )
    owner_ids = jnp.arange(owners, dtype=jnp.int32)
    named = (key_owner[:, :, None] == owner_ids) & (key_live > 0)[:, :, None]
    live = jnp.any(named, axis=1)
    bias = jnp.repeat(jnp.where(live, 0.0, -jnp.inf).astype(F32).T, BLOCK, axis=1)

    quads = heads // QUAD
    by_quad = [kx.reshape(rows, quads, -1), values.reshape(rows, quads, -1)]
    packed = jnp.concatenate(by_quad, axis=2).transpose(1, 0, 2)
    if owners <= 16:
        sums, pulls, row_totals = fused(
            packed, owners, fetch_block[0], qhi, qlo, qraw, out_grad, cott, bias, vecs, head_dim
        )
        summed = sums.transpose(1, 0, 2)
        row_total = jnp.sum(row_totals.reshape(heads, 1, 8, rows), axis=2)
        row_total = jnp.broadcast_to(row_total, (heads, HEAD_COLS, rows)).reshape(-1, rows)
        qgrad = (
            vecs[0].reshape(-1, 1) * pulls.reshape(-1, rows)
            - vecs[1].reshape(-1, 1) * row_total * qt.astype(F32)
        )
    else:
        gathered = gather(packed, owners)
        terms, qgrad = attention(
            gathered, fetch_block[0], qhi, qlo, qraw, out_grad, cott, qt, bias, vecs, head_dim
        )
        summed = scatter_sum(terms).transpose(1, 0, 2)
    query_grad, query_point_grad = unlayout(qgrad.T, heads, head_dim, count)
    split = QUAD * HEAD_COLS
    key_grad, key_point_grad = unlayout(summed[:, :, :split], heads, head_dim, count)
    return query_grad, query_point_grad, key_grad, key_point_grad, summed[:, :, split:].reshape(rows, width)


def solution(mesh):
    rows = P(("grp", "res"), None)
    return jax.shard_map(
        local,
        mesh=mesh,
        in_specs=(rows,) * 5 + (P(),) + (rows,) * 4,
        out_specs=(rows,) * 5,
        check_vma=False,
    )
```
